768 devices in a mesh: node: 12 (over x, z_hi), local: 64 (over y, z_lo, core).
Axes of the slice: x: 4, y: 8, z: 12 (z_hi: 3, z_lo: 4; z = z_hi * 4 + z_lo), core: 2. Of those that a mesh axis runs over, the one named last changes fastest.
Arguments:
- tokens: bfloat16 [196608, 8192], P(('node', 'local')), may hold values from -6 to 6
- cotangent: bfloat16 [196608, 128], P(('node', 'local')), may hold values from -0.013671875 to 0.013671875
- weight_codes: bfloat16 [8192, 128], P('local'), may hold values from -127 to 127, as said below
- weight_scales: bfloat16 [4096], P('local'), may hold values from 4.9829483e-05 to 0.00049972534
- rounding_table: int32 [8192, 128], replicated, may hold values from 0 to 1023
- stream_offsets: int32 [768], P(('node', 'local')), may hold values from 0 to 1023
Outputs:
- projected: bfloat16 [196608, 128], P(('node', 'local'))
- weight_grad: float32 [8192, 128], P('local')
The draws below stay inside these ranges and needn't reach their ends.
Inputs may be any that keep to these rules, and one draw needn't show every extreme that they name: `weight_codes`: whole numbers.
All inputs are finite; a program needn't handle non-finite values.
Results may differ from the reference program's by a relative error of at most 0.012.
Values may be sent and summed in bfloat16 or wider, within the bound.
A program may use at most 64 MiB of HBM per device.

```python
import math
import jax
import jax.numpy as jnp
from jax import lax

D = 8192
HD = 128
QB = 256
TOK_DEV = 256
TOKENS = 196608
N_NODE = 12
N_LOCAL = 64


def draw_weight_codes(key, part):
    key = jax.random.fold_in(key, 11)
    whole = jax.random.randint(key, (D, HD), -127, 128)
    return whole.astype(jnp.float32).astype(jnp.bfloat16)


def place_ends(entries, stream_key, least, high):
    place = [jax.random.randint(jax.random.fold_in(stream_key, axis), (), 0, length) for axis, length in enumerate(entries.shape)]
    widest = entries.shape.index(max(entries.shape))
    beside = place[:widest] + [(place[widest] + 1) % entries.shape[widest]] + place[widest + 1:]
    return entries.at[tuple(place)].set(least).at[tuple(beside)].set(high)


def block_scale(rng, extent, pieces, smallest, top_value):
    level, own = 1.0, jax.random.fold_in(rng, 6)
    for axis_at, blocks in pieces:
        draws = jnp.exp(jax.random.uniform(jax.random.fold_in(own, axis_at), (blocks,), jnp.float32, smallest / len(pieces), top_value / len(pieces)))
        level = level * jnp.repeat(draws, extent[axis_at] // blocks).reshape([-1 if axis == axis_at else 1 for axis in range(len(extent))])
    return level


def gaussian(key, shape, spread, most, cuts=(), kind=jnp.bfloat16):
    values = jax.random.normal(key, shape, jnp.float32) * spread
    if len(cuts) > 0:
        values = block_scale(key, shape, cuts, -0.22, 0.18) * values
    return jnp.clip(values, min=-most, max=most).astype(kind)


def setup_inputs(seed: int = 0) -> dict:
    key_list = jax.random.split(jax.random.key(seed), 7)
    tokens = gaussian(key_list[0], (TOKENS, D), 1.0, 6.0, ((0, 768),))
    cotangent = gaussian(key_list[1], (TOKENS, HD), TOKENS ** -0.5, 0.013671875, ((0, 768),))
    weight_codes = draw_weight_codes(jax.random.fold_in(key_list[6], 71), 0)
    weight_scales = jnp.clip(jnp.exp(math.log(0.00049972534) - 2.3054518 * jax.random.uniform(key_list[3], (D // (QB // HD),), jnp.float32) ** block_scale(key_list[3], (D // (QB // HD),), ((0, 64),), -0.2, 0.2)), 4.982948303222656e-05, 0.00049972534).astype(jnp.bfloat16)
    rounding_table = place_ends(jax.random.randint(key_list[4], (D, HD), 0, 1024), jax.random.fold_in(key_list[4], 1), 0, 1023).astype(jnp.int32)
    stream_offsets = place_ends(jax.random.randint(key_list[5], (N_NODE * N_LOCAL,), 0, 1024), jax.random.fold_in(key_list[5], 1), 0, 1023).astype(jnp.int32)
    return dict(tokens=tokens, cotangent=cotangent, weight_codes=weight_codes, weight_scales=weight_scales, rounding_table=rounding_table, stream_offsets=stream_offsets)


EPS = 1e-6
HEADROOM = 1.0078125
GRAD_TOP = 7.0
NODE_TOP = 127.0


def quantize(blocks, shift, top):
    largest = jnp.max(jnp.abs(blocks), axis=1)
    scale = ((largest + EPS) * HEADROOM / top).astype(jnp.bfloat16)
    codes = (blocks / scale.astype(jnp.float32)[:, None] + (shift - 0.5)).astype(jnp.bfloat16)
    return codes, scale


def dequantize(codes, scale):
    return codes.astype(jnp.float32) * scale.astype(jnp.float32)[:, None]


def dither(table, offset):
    return (jnp.remainder(table + offset, 1024).astype(jnp.float32) + 0.5) / 1024.0


def reference(tokens, cotangent, weight_codes, weight_scales, rounding_table, stream_offsets):
    group = QB // HD
    dense = dequantize(weight_codes.reshape(D // group, QB), weight_scales).astype(jnp.bfloat16).reshape(D, HD)
    projected = jnp.dot(tokens, dense, preferred_element_type=jnp.float32).astype(jnp.bfloat16)
    rows = tokens.reshape(N_NODE, N_LOCAL, TOK_DEV, D)
    grads = cotangent.reshape(N_NODE, N_LOCAL, TOK_DEV, HD)
    offsets = stream_offsets.reshape(N_NODE, N_LOCAL)

    def node_step(total, triple):
        def local_step(acc, item):
            left, right, offset = item
            partial_value = jnp.dot(left.T, right, preferred_element_type=jnp.float32)
            shift = dither(rounding_table, offset).reshape(D // group, QB)
            codes, scale = quantize(partial_value.reshape(D // group, QB), shift, GRAD_TOP)
            return acc + dequantize(codes, scale), None

        start = jnp.zeros((D // group, QB), jnp.float32)
        node_total, unused = lax.scan(local_step, start, triple)
        codes, scale = quantize(node_total, 0.5, NODE_TOP)
        return total + dequantize(codes, scale), None

    begin = jnp.zeros((D // group, QB), jnp.float32)
    total, unused = lax.scan(node_step, begin, (rows, grads, offsets))
    return projected, total.reshape(D, HD)
```

```python
import jax
import jax.numpy as jnp
from jax import lax
from jax.experimental import pallas as pl
from jax.experimental.pallas import tpu as pltpu
from jax.sharding import PartitionSpec as P

MESH = pl.DeviceIdType.MESH
EPS = 1e-06
HEADROOM = 1.0078125
GRAD_TOP = 7.0
NODE_TOP = 127.0

NX, NZH, NY, NZ = 4, 3, 8, 4
HALF_Y = NY // 2
ROWS = 128
HD = 128
HB = ROWS // 2
CHUNK = NZ * 2 * ROWS
TOK = 256


def block_scale(even, odd, top):
    largest = jnp.max(jnp.maximum(jnp.abs(even), jnp.abs(odd)), axis=1, keepdims=True)
    return ((largest + EPS) * HEADROOM / top).astype(jnp.bfloat16).astype(jnp.float32)


def kernel(
    tok_hbm, cot_hbm, wc_hbm, ws_ref, table_hbm, off_ref,
    proj_ref, grad_ref,
    tok, cot, wc, table, part, own, sib_out, sib_in, r_out, r_in, l_out, l_in,
    z_out, z_in, h_buf, x_buf, w_buf,
    tok_sem, table_sem, small_sem, sib_ss, sib_rs, r_ss, r_rs, l_ss, l_rs,
    z_ss, z_rs, h_ss, h_rs, x_ss, x_rs, gz_ss, gz_rs, gr_ss, gr_rs, gl_ss, gl_rs, gs_ss, gs_rs,
):
    node = lax.axis_index("node")
    local = lax.axis_index("local")
    x, zh = node // NZH, node % NZH
    y, z, core = local // (NZ * 2), (local // 2) % NZ, local % 2
    other = 1 - core

    def at(y_, z_, c_):
        return (node, (y_ * NZ + z_) * 2 + c_)

    sibling = at(y, z, other)
    right = at((y + 1) % NY, z, core)
    left = at((y + NY - 1) % NY, z, core)
    z_peers = [at(y, (z + j) % NZ, core) for j in range(1, NZ)]
    h_peers = [(x * NZH + (zh + j) % NZH, local) for j in range(1, NZH)]
    x_peers = [(((x + j) % NX) * NZH + zh, local) for j in range(1, NX)]
    everyone = [sibling, right, left] + z_peers + h_peers + x_peers

    barrier = pltpu.get_barrier_semaphore()
    for peer in everyone:
        pl.semaphore_signal(barrier, inc=1, device_id=peer, device_id_type=MESH)

    order = [(y + HALF_Y) % NY]
    for far in range(HALF_Y - 1, 0, -1):
        order += [(y + far) % NY, (y + NY - far) % NY]
    order += [y]

    def tok_copy(k):
        cols = pl.ds(pl.multiple_of(order[k] * CHUNK, CHUNK), CHUNK)
        return pltpu.make_async_copy(tok_hbm.at[:, cols], tok.at[:, cols], tok_sem.at[k])

    def table_copy(k):
        rows = pl.ds(pl.multiple_of(order[k] * CHUNK, CHUNK), CHUNK)
        return pltpu.make_async_copy(table_hbm.at[rows], table.at[rows], table_sem.at[k])

    cot_copy = pltpu.make_async_copy(cot_hbm, cot, small_sem.at[0])
    wc_copy = pltpu.make_async_copy(wc_hbm, wc, small_sem.at[1])
    cot_copy.start()
    wc_copy.start()
    for k in range(NY):
        tok_copy(k).start()
        table_copy(k).start()

    def remote(src, dst, ss, rs, dev):
        return pltpu.make_async_remote_copy(
            src_ref=src, dst_ref=dst, send_sem=ss, recv_sem=rs, device_id=dev, device_id_type=MESH
        )

    wc_copy.wait()
    row = lax.broadcasted_iota(jnp.int32, (ROWS, HB), 0)
    col = lax.broadcasted_iota(jnp.int32, (ROWS, HB), 1)
    spread = jnp.broadcast_to(ws_ref[...].astype(jnp.float32), (ROWS, HB))
    w_scale = jnp.sum(jnp.where(row // 2 == col, spread, 0.0), axis=1, keepdims=True)
    w_buf[y, z, core] = (wc[...].astype(jnp.float32) * w_scale).astype(jnp.bfloat16)

    pl.semaphore_wait(barrier, len(everyone))

    mine = w_buf.at[y, z, core]
    gz = [remote(mine, mine, gz_ss.at[j], gz_rs.at[j], z_peers[j]) for j in range(NZ - 1)]
    for copy in gz:
        copy.start()

    offset = off_ref[0]
    cot_copy.wait()

    def quantized(block, core_of, base):
        start = pl.multiple_of((block * 2 + core_of) * ROWS, ROWS)
        even = part[pl.ds(start, HB, stride=2), :]
        odd = part[pl.ds(start + 1, HB, stride=2), :]
        scale = block_scale(even, odd, GRAD_TOP)
        inverse = 1.0 / scale
        out = []
        for parity, value in ((0, even), (1, odd)):
            draws = table[pl.ds(base + start + parity, HB, stride=2), :]
            draws = ((draws + offset) & 1023).astype(jnp.float32)
            shift = draws * (1.0 / 1024.0) + (0.5 / 1024.0 - 0.5)
            codes = (value * inverse + shift).astype(jnp.bfloat16)
            out.append(codes.astype(jnp.float32) * scale)
        return out

    def sib_copy(k):
        return remote(sib_out.at[k], sib_in.at[k], sib_ss.at[k], sib_rs.at[k], sibling)

    def compute(k):
        tok_copy(k).wait()
        table_copy(k).wait()
        base = pl.multiple_of(order[k] * CHUNK, CHUNK)
        part[...] = lax.dot_general(
            tok[:, pl.ds(base, CHUNK)], cot[...], (((0,), (0,)), ((), ())),
            preferred_element_type=jnp.float32,
        )
        for block in range(NZ):
            even, odd = quantized(block, other, base)
            sib_out[k, block, :HB] = even.astype(jnp.bfloat16)
            sib_out[k, block, HB:] = odd.astype(jnp.bfloat16)
        sib_copy(k).start()
        for block in range(NZ):
            even, odd = quantized(block, core, base)
            own[k, block, :HB] = even
            own[k, block, HB:] = odd

    def chip_sum(k):
        sib_copy(k).wait_recv()
        return own[k] + sib_in[k].astype(jnp.float32)

    HALF_Z = NZ // 2

    def r_copy(s):
        if s == 0:
            return remote(r_out.at[0, :HALF_Z], r_in.at[0, :HALF_Z], r_ss.at[0], r_rs.at[0], right)
        return remote(r_out.at[s], r_in.at[s], r_ss.at[s], r_rs.at[s], right)

    def l_copy(s):
        if s == 0:
            return remote(l_out.at[0, HALF_Z:], l_in.at[0, HALF_Z:], l_ss.at[0], l_rs.at[0], left)
        return remote(l_out.at[s], l_in.at[s], l_ss.at[s], l_rs.at[s], left)

    def pass_on(k):
        if k == 0:
            total = chip_sum(0).astype(jnp.bfloat16)
            r_out[0, :HALF_Z] = total[:HALF_Z]
            l_out[0, HALF_Z:] = total[HALF_Z:]
            r_copy(0).start()
            l_copy(0).start()
            return
        s = (k + 1) // 2
        total = chip_sum(k)
        copy, out, came = (r_copy, r_out, r_in) if k % 2 == 1 else (l_copy, l_out, l_in)
        copy(s - 1).wait_recv()
        if s == 1:
            low, high = (HALF_Z, NZ) if k % 2 == 1 else (0, HALF_Z)
            joined = (0, HALF_Z) if k % 2 == 1 else (HALF_Z, NZ)
            a, b = joined
            out[s, a:b] = (total[a:b] + came[0, a:b].astype(jnp.float32)).astype(jnp.bfloat16)
            out[s, low:high] = total[low:high].astype(jnp.bfloat16)
        else:
            out[s] = (total + came[s - 1].astype(jnp.float32)).astype(jnp.bfloat16)
        copy(s).start()

    for k in range(NY):
        compute(k)
        if k >= 1:
            pass_on(k - 1)

    def g_copy(way, s):
        if way == 0:
            b, ss, rs, dev = (y + NY - s) % NY, gr_ss, gr_rs, right
        else:
            b, ss, rs, dev = (y + s) % NY, gl_ss, gl_rs, left
        if s == HALF_Y - 1:
            src = w_buf.at[b, :HALF_Z, core] if way == 0 else w_buf.at[b, HALF_Z:, core]
        else:
            src = w_buf.at[b, :, core]
        return remote(src, src, ss.at[s], rs.at[s], dev)

    def g_came(way, s):
        if way == 0:
            b, ss, rs = (y + NY - s - 1) % NY, gr_ss, gr_rs
        else:
            b, ss, rs = (y + s + 1) % NY, gl_ss, gl_rs
        if s == HALF_Y - 1:
            dst = w_buf.at[b, :HALF_Z, core] if way == 0 else w_buf.at[b, HALF_Z:, core]
        else:
            dst = w_buf.at[b, :, core]
        return remote(dst, dst, ss.at[s], rs.at[s], sibling)

    def gs_copy(r):
        src = w_buf.at[(y + r) % NY, :, core]
        return remote(src, src, gs_ss.at[r], gs_rs.at[r], sibling)

    def gs_came(r):
        dst = w_buf.at[(y + r) % NY, :, other]
        return remote(dst, dst, gs_ss.at[r], gs_rs.at[r], sibling)

    for j in range(NZ - 1):
        src = w_buf.at[y, (z + NZ - 1 - j) % NZ, core]
        remote(src, src, gz_ss.at[j], gz_rs.at[j], sibling).wait_recv()
    g_copy(0, 0).start()
    g_copy(1, 0).start()
    gs_copy(0).start()

    total = chip_sum(NY - 1)
    r_copy(HALF_Y - 1).wait_recv()
    total += r_in[HALF_Y - 1].astype(jnp.float32)
    l_copy(HALF_Y - 1).wait_recv()
    total += l_in[HALF_Y - 1].astype(jnp.float32)
    own[NY - 1] = total
    z_out[...] = total.astype(jnp.bfloat16)

    def z_copy(j):
        return remote(
            z_out.at[(z + j + 1) % NZ], z_in.at[j], z_ss.at[j], z_rs.at[j], z_peers[j]
        )

    for j in range(NZ - 1):
        z_copy(j).start()

    def g_step(s):
        g_came(0, s).wait_recv()
        g_came(1, s).wait_recv()
        if s < HALF_Y - 1:
            g_copy(0, s + 1).start()
            g_copy(1, s + 1).start()
            gs_copy(NY - s - 1).start()
            gs_copy(s + 1).start()
        else:
            gs_copy(HALF_Y).start()

    g_step(0)

    node_total = own[NY - 1, z]
    for j in range(NZ - 1):
        z_copy(j).wait_recv()
        node_total += z_in[j].astype(jnp.float32)
    even, odd = node_total[:HB], node_total[HB:]
    scale = block_scale(even, odd, NODE_TOP)
    inverse = 1.0 / scale
    for at_row, value in ((0, even), (HB, odd)):
        codes = (value * inverse).astype(jnp.bfloat16)
        h_buf[zh, at_row:at_row + HB] = (codes.astype(jnp.float32) * scale).astype(jnp.bfloat16)

    def h_copy(j):
        return remote(h_buf.at[zh], h_buf.at[zh], h_ss.at[j], h_rs.at[j], h_peers[j])

    def h_came(j):
        dst = h_buf.at[(zh + NZH - 1 - j) % NZH]
        return remote(dst, dst, h_ss.at[j], h_rs.at[j], sibling)

    for j in range(NZH - 1):
        h_copy(j).start()

    g_step(1)

    for j in range(NZH - 1):
        h_came(j).wait_recv()
    summed = h_buf[0].astype(jnp.float32)
    for i in range(1, NZH):
        summed += h_buf[i].astype(jnp.float32)
    x_buf[x] = summed.astype(jnp.bfloat16)

    def x_copy(j):
        return remote(x_buf.at[x], x_buf.at[x], x_ss.at[j], x_rs.at[j], x_peers[j])

    def x_came(j):
        dst = x_buf.at[(x + NX - 1 - j) % NX]
        return remote(dst, dst, x_ss.at[j], x_rs.at[j], sibling)

    for j in range(NX - 1):
        x_copy(j).start()

    g_step(2)

    def term(r):
        gs_came(r).wait_recv()
        b = (y + r) % NY
        dense = w_buf[b].reshape(CHUNK, HD)
        cols = pl.ds(pl.multiple_of(b * CHUNK, CHUNK), CHUNK)
        return jnp.dot(tok[:, cols], dense, preferred_element_type=jnp.float32)

    projected = term(0)
    for s in range(1, HALF_Y - 1):
        projected += term(s)
        projected += term(NY - s)

    for j in range(NX - 1):
        x_came(j).wait_recv()
    summed = x_buf[0].astype(jnp.float32)
    for i in range(1, NX):
        summed += x_buf[i].astype(jnp.float32)
    grad_ref[pl.ds(0, HB, stride=2), :] = summed[:HB]
    grad_ref[pl.ds(1, HB, stride=2), :] = summed[HB:]

    g_step(HALF_Y - 1)
    projected += term(HALF_Y - 1)
    projected += term(HALF_Y + 1)
    projected += term(HALF_Y)
    proj_ref[...] = projected.astype(jnp.bfloat16)

    for copy in gz:
        copy.wait_send()
    for k in range(NY):
        sib_copy(k).wait_send()
        gs_copy(k).wait_send()
    for s in range(HALF_Y):
        r_copy(s).wait_send()
        l_copy(s).wait_send()
        g_copy(0, s).wait_send()
        g_copy(1, s).wait_send()
    for j in range(NZ - 1):
        z_copy(j).wait_send()
    for j in range(NZH - 1):
        h_copy(j).wait_send()
    for j in range(NX - 1):
        x_copy(j).wait_send()


def on_device(tokens, cotangent, weight_codes, weight_scales, rounding_table, stream_offsets):
    dma = pltpu.SemaphoreType.DMA
    bf16, f32 = jnp.bfloat16, jnp.float32
    column = (NZ, ROWS, HD)
    scratch = [
        pltpu.VMEM((TOK, NY * CHUNK), bf16),
        pltpu.VMEM((TOK, HD), bf16),
        pltpu.VMEM((ROWS, HD), bf16),
        pltpu.VMEM((NY * CHUNK, HD), jnp.int32),
        pltpu.VMEM((CHUNK, HD), f32),
        pltpu.VMEM((NY,) + column, f32),
        pltpu.VMEM((NY,) + column, bf16),
        pltpu.VMEM((NY,) + column, bf16),
        pltpu.VMEM((HALF_Y,) + column, bf16),
        pltpu.VMEM((HALF_Y,) + column, bf16),
        pltpu.VMEM((HALF_Y,) + column, bf16),
        pltpu.VMEM((HALF_Y,) + column, bf16),
        pltpu.VMEM(column, bf16),
        pltpu.VMEM((NZ - 1, ROWS, HD), bf16),
        pltpu.VMEM((NZH, ROWS, HD), bf16),
        pltpu.VMEM((NX, ROWS, HD), bf16),
        pltpu.VMEM((NY, NZ, 2, ROWS, HD), bf16),
        dma((NY,)), dma((NY,)), dma((2,)), dma((NY,)), dma((NY,)),
        dma((HALF_Y,)), dma((HALF_Y,)), dma((HALF_Y,)), dma((HALF_Y,)),
        dma((NZ - 1,)), dma((NZ - 1,)), dma((NZH - 1,)), dma((NZH - 1,)),
        dma((NX - 1,)), dma((NX - 1,)), dma((NZ - 1,)), dma((NZ - 1,)),
        dma((HALF_Y,)), dma((HALF_Y,)), dma((HALF_Y,)), dma((HALF_Y,)),
        dma((NY,)), dma((NY,)),
    ]
    anywhere = pl.BlockSpec(memory_space=pl.ANY)
    vmem = pl.BlockSpec(memory_space=pltpu.VMEM)
    return pl.pallas_call(
        kernel,
        out_shape=(
            jax.ShapeDtypeStruct((TOK, HD), bf16),
            jax.ShapeDtypeStruct((ROWS, HD), f32),
        ),
        in_specs=[anywhere, anywhere, anywhere, vmem, anywhere,
                  pl.BlockSpec(memory_space=pltpu.SMEM)],
        out_specs=(vmem, vmem),
        scratch_shapes=scratch,
        compiler_params=pltpu.CompilerParams(
            collective_id=0, has_side_effects=True, vmem_limit_bytes=48 * 2**20
        ),
        cost_estimate=pl.CostEstimate(
            flops=4 * TOK * NY * CHUNK * HD, bytes_accessed=9 * 2**20, transcendentals=0
        ),
    )(tokens, cotangent, weight_codes, weight_scales.reshape(1, HB), rounding_table, stream_offsets)


def solution(mesh):
    assert dict(mesh.shape) == {"node": NX * NZH, "local": NY * NZ * 2}
    in_specs = (
        P(("node", "local"), None),
        P(("node", "local"), None),
        P("local", None),
        P("local"),
        P(),
        P(("node", "local")),
    )
    out_specs = (P(("node", "local"), None), P("local", None))
    return jax.shard_map(
        on_device, mesh=mesh, in_specs=in_specs, out_specs=out_specs, check_vma=False
    )
```

```python
import jax
import jax.numpy as jnp
from jax import lax
from jax.experimental import pallas as pl
from jax.experimental.pallas import tpu as pltpu
from jax.sharding import PartitionSpec as P

MESH = pl.DeviceIdType.MESH
EPS = 1e-06
HEADROOM = 1.0078125
GRAD_TOP = 7.0
NODE_TOP = 127.0

NX, NZH, NY, NZ = 4, 3, 8, 4
HALF_Y = NY // 2
ROWS = 128
HD = 128
HB = ROWS // 2
CHUNK = NZ * 2 * ROWS
TOK = 256
HALF_Z = NZ // 2
VMEM_LIMIT = 60 * 2**20
AHEAD = 3


def block_scale(even, odd, top):
    largest = jnp.max(jnp.maximum(jnp.abs(even), jnp.abs(odd)), axis=1, keepdims=True)
    return ((largest + EPS) * HEADROOM / top).astype(jnp.bfloat16).astype(jnp.float32)


def kernel(
    tok_hbm, cot_hbm, wc_hbm, ws_hbm, table_hbm, off_ref,
    proj_ref, grad_ref,
    tok, cot, wc, ws, table, part, own, sib_out, sib_in, r_out, r_in, l_out, l_in,
    z_out, z_in, h_buf, x_buf, w_buf,
    tok_sem, table_sem, small_sem, sib_ss, sib_rs, r_ss, r_rs, l_ss, l_rs,
    z_ss, z_rs, h_ss, h_rs, x_ss, x_rs, gz_ss, gz_rs, gr_ss, gr_rs, gl_ss, gl_rs,
    gx_ss, gx_rs, gs_ss, gs_rs, later_h,
):
    node = lax.axis_index("node")
    local = lax.axis_index("local")
    x, zh = node // NZH, node % NZH
    y, z, core = local // (NZ * 2), (local // 2) % NZ, local % 2
    other = 1 - core

    def at(y_, z_, c_):
        return (node, (y_ * NZ + z_) * 2 + c_)

    def up(step):
        return at((y + step) % NY, z, core)

    def down(step):
        return at((y + NY - step) % NY, z, core)

    sibling = at(y, z, other)
    x_peers = [(((x + j) % NX) * NZH + zh, local) for j in range(1, NX)]
    z_peers = [at(y, (z + j) % NZ, core) for j in range(1, NZ)]
    near = [sibling, up(1), down(1)] + z_peers + x_peers

    def h_peer(zh_):
        return (x * NZH + zh_, local)

    def signal(sem, peer):
        pl.semaphore_signal(sem, inc=1, device_id=peer, device_id_type=MESH)

    barrier = pltpu.get_barrier_semaphore()
    for peer in near:
        signal(barrier, peer)
    for zh_ in range(1, NZH):
        @pl.when(zh < zh_)
        def _():
            signal(barrier, h_peer(zh_))

    order = [(y + HALF_Y) % NY]
    for far in range(HALF_Y - 1, 0, -1):
        order += [(y + far) % NY, (y + NY - far) % NY]
    order += [y]

    def tok_copy(k):
        cols = pl.ds(pl.multiple_of(order[k] * CHUNK, CHUNK), CHUNK)
        return pltpu.make_async_copy(tok_hbm.at[:, cols], tok.at[:, cols], tok_sem.at[k])

    def table_copy(k):
        rows = pl.ds(pl.multiple_of(order[k] * CHUNK, CHUNK), CHUNK)
        return pltpu.make_async_copy(table_hbm.at[rows], table.at[rows], table_sem.at[k])

    def fetch(k):
        tok_copy(k).start()
        table_copy(k).start()

    cot_copy = pltpu.make_async_copy(cot_hbm, cot, small_sem.at[0])
    wc_copy = pltpu.make_async_copy(wc_hbm, wc, small_sem.at[1])
    ws_copy = pltpu.make_async_copy(ws_hbm, ws, small_sem.at[2])
    cot_copy.start()
    fetch(0)
    wc_copy.start()
    ws_copy.start()
    for k in range(1, AHEAD):
        fetch(k)

    def remote(src, dst, ss, rs, dev):
        return pltpu.make_async_remote_copy(
            src_ref=src, dst_ref=dst, send_sem=ss, recv_sem=rs, device_id=dev, device_id_type=MESH
        )

    offset = off_ref[0]

    def quantized(block, core_of, base):
        start = pl.multiple_of((block * 2 + core_of) * ROWS, ROWS)
        even = part[pl.ds(start, HB, stride=2), :]
        odd = part[pl.ds(start + 1, HB, stride=2), :]
        scale = block_scale(even, odd, GRAD_TOP)
        inverse = 1.0 / scale
        out = []
        for parity, value in ((0, even), (1, odd)):
            draws = table[pl.ds(base + start + parity, HB, stride=2), :]
            draws = ((draws + offset) & 1023).astype(jnp.float32)
            shift = draws * (1.0 / 1024.0) + (0.5 / 1024.0 - 0.5)
            codes = (value * inverse + shift).astype(jnp.bfloat16)
            out.append(codes.astype(jnp.float32) * scale)
        return out

    def sib_copy(k):
        return remote(sib_out.at[k], sib_in.at[k], sib_ss.at[k], sib_rs.at[k], sibling)

    def compute(k, ready=None):
        tok_copy(k).wait()
        table_copy(k).wait()
        if k + AHEAD < NY:
            fetch(k + AHEAD)
        base = pl.multiple_of(order[k] * CHUNK, CHUNK)
        part[...] = lax.dot_general(
            tok[:, pl.ds(base, CHUNK)], cot[...], (((0,), (0,)), ((), ())),
            preferred_element_type=jnp.float32,
        )
        for block in range(NZ):
            even, odd = quantized(block, other, base)
            sib_out[k, block, :HB] = even.astype(jnp.bfloat16)
            sib_out[k, block, HB:] = odd.astype(jnp.bfloat16)
        if ready is not None:
            ready()
        if k > 0:
            sib_copy(k).start()
        for block in range(NZ):
            even, odd = quantized(block, core, base)
            own[k, block, :HB] = even
            own[k, block, HB:] = odd

    def ring_copy(way, s, q):
        out, came, ss, rs, dev = (
            (r_out, r_in, r_ss, r_rs, up(1)) if way == 0 else (l_out, l_in, l_ss, l_rs, down(1))
        )
        return remote(out.at[s, q], came.at[s, q], ss.at[s, q], rs.at[s, q], dev)

    ways = (range(HALF_Z), range(HALF_Z, NZ))

    def pass_on(way, s, part_of):
        k = 0 if s == 0 else 2 * s - 1 + way
        out, came = (r_out, r_in) if way == 0 else (l_out, l_in)
        for q in ways[part_of]:
            total = own[k, q] + sib_in[k, q].astype(jnp.float32)
            if s > 1 or (s == 1 and part_of == way):
                ring_copy(way, s - 1, q).wait_recv()
                total += came[s - 1, q].astype(jnp.float32)
            out[s, q] = total.astype(jnp.bfloat16)
            ring_copy(way, s, q).start()

    def gz_copy(j):
        piece = w_buf.at[y, z, core, x]
        return remote(piece, piece, gz_ss.at[j], gz_rs.at[j], z_peers[j])

    def gz_came(j):
        piece = w_buf.at[y, (z + NZ - 1 - j) % NZ, core, x]
        return remote(piece, piece, gz_ss.at[j], gz_rs.at[j], sibling)

    def gy_copy(way, s):
        if way == 0:
            piece = w_buf.at[(y + NY - s) % NY, :, core, x]
            return remote(piece, piece, gr_ss.at[s], gr_rs.at[s], up(1))
        piece = w_buf.at[(y + s) % NY, :, core, x]
        return remote(piece, piece, gl_ss.at[s], gl_rs.at[s], down(1))

    def gy_came(way, s):
        if way == 0:
            piece = w_buf.at[(y + NY - s - 1) % NY, :, core, x]
            return remote(piece, piece, gr_ss.at[s], gr_rs.at[s], sibling)
        piece = w_buf.at[(y + s + 1) % NY, :, core, x]
        return remote(piece, piece, gl_ss.at[s], gl_rs.at[s], sibling)

    def gx_copy(r, j):
        piece = w_buf.at[(y + r) % NY, :, core, x]
        return remote(piece, piece, gx_ss.at[r, j], gx_rs.at[r, j], x_peers[j])

    def gx_came(r, j):
        piece = w_buf.at[(y + r) % NY, :, core, (x + NX - 1 - j) % NX]
        return remote(piece, piece, gx_ss.at[r, j], gx_rs.at[r, j], sibling)

    def gs_copy(r):
        piece = w_buf.at[(y + r) % NY, :, core]
        return remote(piece, piece, gs_ss.at[r], gs_rs.at[r], sibling)

    def gs_came(r):
        piece = w_buf.at[(y + r) % NY, :, other]
        return remote(piece, piece, gs_ss.at[r], gs_rs.at[r], sibling)

    def gx_send(r):
        for j in range(NX - 1):
            gx_copy(r, j).start()

    def g_step(s):
        if s >= 0:
            gy_came(0, s).wait_recv()
            if s < HALF_Y - 1:
                gy_came(1, s).wait_recv()
        else:
            for j in range(NZ - 1):
                gz_came(j).wait_recv()
        if s + 1 < HALF_Y:
            gy_copy(0, s + 1).start()
        if s + 1 < HALF_Y - 1:
            gy_copy(1, s + 1).start()
        gx_send((NY - s - 1) % NY)
        if 0 <= s < HALF_Y - 1:
            gx_send(s + 1)

    def to_sibling(rows):
        for r in rows:
            for j in range(NX - 1):
                gx_came(r, j).wait_recv()
            gs_copy(r).start()

    near_rows, far_rows = (0, NY - 1, 1, NY - 2, 2), (NY - 3, 3, HALF_Y)

    wc_copy.wait()
    ws_copy.wait()
    row = lax.broadcasted_iota(jnp.int32, (ROWS, HB), 0)
    col = lax.broadcasted_iota(jnp.int32, (ROWS, HB), 1)
    spread = jnp.broadcast_to(ws[...].astype(jnp.float32), (ROWS, HB))
    w_scale = jnp.sum(jnp.where(row // 2 == col, spread, 0.0), axis=1, keepdims=True)
    wc[...] = (wc[...].astype(jnp.float32) * w_scale).astype(jnp.bfloat16)
    quarter = ROWS // NX
    w_buf[y, z, core, x] = wc[pl.ds(pl.multiple_of(x * quarter, quarter), quarter)]

    def enter():
        pl.semaphore_wait(barrier, len(near) + zh)
        for j in range(NZ - 1):
            gz_copy(j).start()
        for zh_ in range(NZH - 1):
            @pl.when(zh_ < zh)
            def _():
                signal(later_h, h_peer(zh_))

    def first_sends():
        enter()
        sib_copy(0).start()

    cot_copy.wait()
    compute(0)
    compute(1, first_sends)
    sib_copy(0).wait_recv()
    pass_on(0, 0, 0)
    pass_on(1, 0, 1)
    compute(2)
    sib_copy(1).wait_recv()
    pass_on(0, 1, 1)
    compute(3)
    sib_copy(2).wait_recv()
    pass_on(1, 1, 0)
    g_step(-1)
    compute(4)
    sib_copy(3).wait_recv()
    pass_on(0, 1, 0)
    pass_on(1, 1, 1)
    g_step(0)
    compute(5)
    sib_copy(4).wait_recv()
    pass_on(0, 2, 1)
    pass_on(1, 2, 0)
    compute(6)
    sib_copy(5).wait_recv()
    pass_on(0, 2, 0)
    pass_on(1, 2, 1)
    g_step(1)
    compute(7)
    sib_copy(6).wait_recv()
    pass_on(0, 3, 1)
    pass_on(1, 3, 0)
    pass_on(0, 3, 0)
    pass_on(1, 3, 1)
    sib_copy(7).wait_recv()

    g_step(2)

    last = HALF_Y - 1

    def z_copy(z_):
        return remote(z_out.at[z_], z_in.at[z], z_ss.at[z_], z_rs.at[z], at(y, z_, core))

    def z_came(z_):
        return remote(z_out.at[z_], z_in.at[z_], z_ss.at[z_], z_rs.at[z_], sibling)

    for q in range(NZ):
        ring_copy(0, last, q).wait_recv()
        ring_copy(1, last, q).wait_recv()
        total = own[NY - 1, q] + sib_in[NY - 1, q].astype(jnp.float32)
        total += r_in[last, q].astype(jnp.float32) + l_in[last, q].astype(jnp.float32)
        own[NY - 1, q] = total
        z_out[q] = total.astype(jnp.bfloat16)

        @pl.when(q != z)
        def _():
            z_copy(q).start()

    node_total = own[NY - 1, z]
    for j in range(1, NZ):
        z_ = (z + j) % NZ
        z_came(z_).wait_recv()
        node_total += z_in[z_].astype(jnp.float32)
    even, odd = node_total[:HB], node_total[HB:]
    scale = block_scale(even, odd, NODE_TOP)
    inverse = 1.0 / scale
    for at_row, value in ((0, even), (HB, odd)):
        codes = (value * inverse).astype(jnp.bfloat16)
        h_buf[zh, at_row:at_row + HB] = (codes.astype(jnp.float32) * scale).astype(jnp.bfloat16)

    def h_copy(j):
        return remote(
            h_buf.at[zh], h_buf.at[zh], h_ss.at[j], h_rs.at[j], h_peer((zh + j + 1) % NZH)
        )

    def h_came(j):
        dst = h_buf.at[(zh + NZH - 1 - j) % NZH]
        return remote(dst, dst, h_ss.at[j], h_rs.at[j], sibling)

    @pl.when(zh < NZH - 1)
    def _():
        pl.semaphore_wait(later_h, NZH - 1 - zh)

    for j in range(NZH - 1):
        h_copy(j).start()

    g_step(3)
    to_sibling(near_rows)
    to_sibling(far_rows)

    def term(r):
        gs_came(r).wait_recv()
        b = (y + r) % NY
        dense = w_buf[b].reshape(CHUNK, HD)
        cols = pl.ds(pl.multiple_of(b * CHUNK, CHUNK), CHUNK)
        return jnp.dot(tok[:, cols], dense, preferred_element_type=jnp.float32)

    projected = term(0) + term(NY - 1) + term(1)

    for j in range(NZH - 1):
        h_came(j).wait_recv()
    summed = h_buf[0].astype(jnp.float32)
    for i in range(1, NZH):
        summed += h_buf[i].astype(jnp.float32)
    x_buf[x] = summed.astype(jnp.bfloat16)

    def x_copy(j):
        return remote(x_buf.at[x], x_buf.at[x], x_ss.at[j], x_rs.at[j], x_peers[j])

    def x_came(j):
        dst = x_buf.at[(x + NX - 1 - j) % NX]
        return remote(dst, dst, x_ss.at[j], x_rs.at[j], sibling)

    for j in range(NX - 1):
        x_copy(j).start()

    for r in (NY - 2, 2) + far_rows:
        projected += term(r)
    proj_ref[...] = projected.astype(jnp.bfloat16)

    for k in range(NY):
        sib_copy(k).wait_send()
        gs_copy(k).wait_send()
        for j in range(NX - 1):
            gx_copy(k, j).wait_send()
    for s in range(HALF_Y):
        for q in range(NZ):
            for way in range(2):
                if s > 0 or q in ways[way]:
                    ring_copy(way, s, q).wait_send()
    for s in range(HALF_Y):
        gy_copy(0, s).wait_send()
    for s in range(HALF_Y - 1):
        gy_copy(1, s).wait_send()
    for j in range(NZ - 1):
        gz_copy(j).wait_send()
        z_copy((z + j + 1) % NZ).wait_send()
    for j in range(NZH - 1):
        h_copy(j).wait_send()

    for j in range(NX - 1):
        x_came(j).wait_recv()
    summed = x_buf[0].astype(jnp.float32)
    for i in range(1, NX):
        summed += x_buf[i].astype(jnp.float32)
    grad_ref[pl.ds(0, HB, stride=2), :] = summed[:HB]
    grad_ref[pl.ds(1, HB, stride=2), :] = summed[HB:]
    for j in range(NX - 1):
        x_copy(j).wait_send()


def settle(p_ref, g_ref, proj_ref, grad_ref):
    proj_ref[...] = p_ref[...]
    grad_ref[...] = g_ref[...]


def on_device(tokens, cotangent, weight_codes, weight_scales, rounding_table, stream_offsets):
    dma = pltpu.SemaphoreType.DMA
    bf16, f32 = jnp.bfloat16, jnp.float32
    column = (NZ, ROWS, HD)
    scratch = [
        pltpu.VMEM((TOK, NY * CHUNK), bf16),
        pltpu.VMEM((TOK, HD), bf16),
        pltpu.VMEM((ROWS, HD), bf16),
        pltpu.VMEM((1, HB), bf16),
        pltpu.VMEM((NY * CHUNK, HD), jnp.int32),
        pltpu.VMEM((CHUNK, HD), f32),
        pltpu.VMEM((NY,) + column, f32),
        pltpu.VMEM((NY,) + column, bf16),
        pltpu.VMEM((NY,) + column, bf16),
        pltpu.VMEM((HALF_Y,) + column, bf16),
        pltpu.VMEM((HALF_Y,) + column, bf16),
        pltpu.VMEM((HALF_Y,) + column, bf16),
        pltpu.VMEM((HALF_Y,) + column, bf16),
        pltpu.VMEM(column, bf16),
        pltpu.VMEM(column, bf16),
        pltpu.VMEM((NZH, ROWS, HD), bf16),
        pltpu.VMEM((NX, ROWS, HD), bf16),
        pltpu.VMEM((NY, NZ, 2, NX, ROWS // NX, HD), bf16),
        dma((NY,)), dma((NY,)), dma((3,)), dma((NY,)), dma((NY,)),
        dma((HALF_Y, NZ)), dma((HALF_Y, NZ)), dma((HALF_Y, NZ)), dma((HALF_Y, NZ)),
        dma((NZ,)), dma((NZ,)), dma((NZH - 1,)), dma((NZH - 1,)), dma((NX - 1,)), dma((NX - 1,)),
        dma((NZ - 1,)), dma((NZ - 1,)),
        dma((HALF_Y,)), dma((HALF_Y,)), dma((HALF_Y,)), dma((HALF_Y,)),
        dma((NY, NX - 1)), dma((NY, NX - 1)),
        dma((NY,)), dma((NY,)),
        pltpu.SemaphoreType.REGULAR,
    ]
    hbm = pl.BlockSpec(memory_space=pltpu.MemorySpace.HBM)
    vmem = pl.BlockSpec(memory_space=pltpu.VMEM)
    out_shape = (
        jax.ShapeDtypeStruct((TOK, HD), bf16),
        jax.ShapeDtypeStruct((ROWS, HD), f32),
    )
    results = pl.pallas_call(
        kernel,
        out_shape=out_shape,
        in_specs=[hbm, hbm, hbm, hbm, hbm, pl.BlockSpec(memory_space=pltpu.SMEM)],
        out_specs=(vmem, vmem),
        scratch_shapes=scratch,
        compiler_params=pltpu.CompilerParams(
            collective_id=0, has_side_effects=True, vmem_limit_bytes=VMEM_LIMIT
        ),
        cost_estimate=pl.CostEstimate(
            flops=4 * TOK * NY * CHUNK * HD, bytes_accessed=9 * 2**20, transcendentals=0
        ),
    )(tokens, cotangent, weight_codes, weight_scales.reshape(1, HB), rounding_table, stream_offsets)
    return pl.pallas_call(
        settle,
        out_shape=out_shape,
        in_specs=[vmem, vmem],
        out_specs=(vmem, vmem),
        compiler_params=pltpu.CompilerParams(vmem_limit_bytes=VMEM_LIMIT),
    )(*results)


def solution(mesh):
    assert dict(mesh.shape) == {"node": NX * NZH, "local": NY * NZ * 2}
    in_specs = (
        P(("node", "local"), None),
        P(("node", "local"), None),
        P("local", None),
        P("local"),
        P(),
        P(("node", "local")),
    )
    out_specs = (P(("node", "local"), None), P("local", None))
    return jax.shard_map(
        on_device, mesh=mesh, in_specs=in_specs, out_specs=out_specs, check_vma=False
    )
```

```python
import jax
import jax.numpy as jnp
from jax import lax
from jax.experimental import pallas as pl
from jax.experimental.pallas import tpu as pltpu
from jax.sharding import PartitionSpec as P

MESH = pl.DeviceIdType.MESH
EPS = 1e-06
HEADROOM = 1.0078125
GRAD_TOP = 7.0
NODE_TOP = 127.0

NX, NZH, NY, NZ = 4, 3, 8, 4
HALF_Y = NY // 2
ROWS = 128
HD = 128
HB = ROWS // 2
CHUNK = NZ * 2 * ROWS
TOK = 256
HALF_Z = NZ // 2
VMEM_LIMIT = 60 * 2**20
AHEAD = 3


def block_scale(even, odd, top):
    largest = jnp.max(jnp.maximum(jnp.abs(even), jnp.abs(odd)), axis=1, keepdims=True)
    return ((largest + EPS) * HEADROOM / top).astype(jnp.bfloat16).astype(jnp.float32)


def kernel(
    tok_hbm, cot_hbm, wc_hbm, ws_hbm, table_hbm, off_ref,
    proj_ref, grad_ref,
    tok, cot, wc, ws, table, part, own, sib_out, sib_in, r_out, r_in, l_out, l_in,
    z_out, z_in, h_buf, x_buf, w_buf,
    tok_sem, table_sem, small_sem, sib_ss, sib_rs, r_ss, r_rs, l_ss, l_rs,
    z_ss, z_rs, h_ss, h_rs, x_ss, x_rs, gz_ss, gz_rs, gr_ss, gr_rs, gl_ss, gl_rs,
    gx_ss, gx_rs, gs_ss, gs_rs, later_h,
):
    node = lax.axis_index("node")
    local = lax.axis_index("local")
    x, zh = node // NZH, node % NZH
    y, z, core = local // (NZ * 2), (local // 2) % NZ, local % 2
    other = 1 - core

    def at(y_, z_, c_):
        return (node, (y_ * NZ + z_) * 2 + c_)

    def up(step):
        return at((y + step) % NY, z, core)

    def down(step):
        return at((y + NY - step) % NY, z, core)

    sibling = at(y, z, other)
    x_peers = [(((x + j) % NX) * NZH + zh, local) for j in range(1, NX)]
    z_peers = [at(y, (z + j) % NZ, core) for j in range(1, NZ)]
    near = [sibling, up(1), down(1)] + z_peers + x_peers

    def h_peer(zh_):
        return (x * NZH + zh_, local)

    def signal(sem, peer):
        pl.semaphore_signal(sem, inc=1, device_id=peer, device_id_type=MESH)

    barrier = pltpu.get_barrier_semaphore()
    for peer in near:
        signal(barrier, peer)
    for zh_ in range(1, NZH):
        @pl.when(zh < zh_)
        def _():
            signal(barrier, h_peer(zh_))

    order = [(y + HALF_Y) % NY]
    for far in range(HALF_Y - 1, 0, -1):
        order += [(y + far) % NY, (y + NY - far) % NY]
    order += [y]

    def tok_copy(k):
        cols = pl.ds(pl.multiple_of(order[k] * CHUNK, CHUNK), CHUNK)
        return pltpu.make_async_copy(tok_hbm.at[:, cols], tok.at[:, cols], tok_sem.at[k])

    def table_copy(k):
        rows = pl.ds(pl.multiple_of(order[k] * CHUNK, CHUNK), CHUNK)
        return pltpu.make_async_copy(table_hbm.at[rows], table.at[rows], table_sem.at[k])

    def fetch(k):
        tok_copy(k).start()
        table_copy(k).start()

    cot_copy = pltpu.make_async_copy(cot_hbm, cot, small_sem.at[0])
    wc_copy = pltpu.make_async_copy(wc_hbm, wc, small_sem.at[1])
    ws_copy = pltpu.make_async_copy(ws_hbm, ws, small_sem.at[2])
    cot_copy.start()
    fetch(0)
    wc_copy.start()
    ws_copy.start()
    for k in range(1, AHEAD):
        fetch(k)

    def remote(src, dst, ss, rs, dev):
        return pltpu.make_async_remote_copy(
            src_ref=src, dst_ref=dst, send_sem=ss, recv_sem=rs, device_id=dev, device_id_type=MESH
        )

    offset = off_ref[0]

    def quantized(block, core_of, base):
        start = pl.multiple_of((block * 2 + core_of) * ROWS, ROWS)
        even = part[pl.ds(start, HB, stride=2), :]
        odd = part[pl.ds(start + 1, HB, stride=2), :]
        scale = block_scale(even, odd, GRAD_TOP)
        inverse = 1.0 / scale
        out = []
        for parity, value in ((0, even), (1, odd)):
            draws = table[pl.ds(base + start + parity, HB, stride=2), :]
            draws = ((draws + offset) & 1023).astype(jnp.float32)
            shift = draws * (1.0 / 1024.0) + (0.5 / 1024.0 - 0.5)
            codes = (value * inverse + shift).astype(jnp.bfloat16)
            out.append(codes.astype(jnp.float32) * scale)
        return out

    def sib_copy(k):
        return remote(sib_out.at[k], sib_in.at[k], sib_ss.at[k], sib_rs.at[k], sibling)

    def compute(k, ready=None):
        tok_copy(k).wait()
        table_copy(k).wait()
        if k + AHEAD < NY:
            fetch(k + AHEAD)
        base = pl.multiple_of(order[k] * CHUNK, CHUNK)
        part[...] = lax.dot_general(
            tok[:, pl.ds(base, CHUNK)], cot[...], (((0,), (0,)), ((), ())),
            preferred_element_type=jnp.float32,
        )
        for block in range(NZ):
            even, odd = quantized(block, other, base)
            sib_out[k, block, :HB] = even.astype(jnp.bfloat16)
            sib_out[k, block, HB:] = odd.astype(jnp.bfloat16)
        if ready is not None:
            ready()
        if k > 0:
            sib_copy(k).start()
        for block in range(NZ):
            even, odd = quantized(block, core, base)
            own[k, block, :HB] = even
            own[k, block, HB:] = odd

    def ring_copy(way, s, q):
        out, came, ss, rs, dev = (
            (r_out, r_in, r_ss, r_rs, up(1)) if way == 0 else (l_out, l_in, l_ss, l_rs, down(1))
        )
        return remote(out.at[s, q], came.at[s, q], ss.at[s, q], rs.at[s, q], dev)

    ways = (range(HALF_Z), range(HALF_Z, NZ))

    def pass_on(way, s, part_of):
        k = 0 if s == 0 else 2 * s - 1 + way
        out, came = (r_out, r_in) if way == 0 else (l_out, l_in)
        for q in ways[part_of]:
            total = own[k, q] + sib_in[k, q].astype(jnp.float32)
            if s > 1 or (s == 1 and part_of == way):
                ring_copy(way, s - 1, q).wait_recv()
                total += came[s - 1, q].astype(jnp.float32)
            out[s, q] = total.astype(jnp.bfloat16)
            ring_copy(way, s, q).start()

    def gy_copy(way, s):
        if way == 0:
            piece = w_buf.at[(y + NY - s) % NY, z, core, x]
            return remote(piece, piece, gr_ss.at[s], gr_rs.at[s], up(1))
        piece = w_buf.at[(y + s) % NY, z, core, x]
        return remote(piece, piece, gl_ss.at[s], gl_rs.at[s], down(1))

    def gy_came(way, s):
        if way == 0:
            piece = w_buf.at[(y + NY - s - 1) % NY, z, core, x]
            return remote(piece, piece, gr_ss.at[s], gr_rs.at[s], sibling)
        piece = w_buf.at[(y + s + 1) % NY, z, core, x]
        return remote(piece, piece, gl_ss.at[s], gl_rs.at[s], sibling)

    def gz_copy(r, j):
        piece = w_buf.at[(y + r) % NY, z, core, x]
        return remote(piece, piece, gz_ss.at[r, j], gz_rs.at[r, j], z_peers[j])

    def gz_came(r, j):
        piece = w_buf.at[(y + r) % NY, (z + NZ - 1 - j) % NZ, core, x]
        return remote(piece, piece, gz_ss.at[r, j], gz_rs.at[r, j], sibling)

    def gx_copy(r, j):
        piece = w_buf.at[(y + r) % NY, :, core, x]
        return remote(piece, piece, gx_ss.at[r, j], gx_rs.at[r, j], x_peers[j])

    def gx_came(r, j):
        piece = w_buf.at[(y + r) % NY, :, core, (x + NX - 1 - j) % NX]
        return remote(piece, piece, gx_ss.at[r, j], gx_rs.at[r, j], sibling)

    def gs_copy(r):
        piece = w_buf.at[(y + r) % NY, :, core]
        return remote(piece, piece, gs_ss.at[r], gs_rs.at[r], sibling)

    def gs_came(r):
        piece = w_buf.at[(y + r) % NY, :, other]
        return remote(piece, piece, gs_ss.at[r], gs_rs.at[r], sibling)

    def along_y(s):
        if s < HALF_Y:
            gy_copy(0, s).start()
        if s < HALF_Y - 1:
            gy_copy(1, s).start()

    def along_z(rows):
        for r in rows:
            for j in range(NZ - 1):
                gz_copy(r, j).start()

    def along_x(rows):
        for r in rows:
            for j in range(NZ - 1):
                gz_came(r, j).wait_recv()
            for j in range(NX - 1):
                gx_copy(r, j).start()

    near_rows, far_rows = (0, NY - 1, 1, NY - 2, 2), (NY - 3, 3, HALF_Y)

    came_at = ((0,), (NY - 1, 1), (NY - 2, 2), (NY - 3, 3), (HALF_Y,))

    def g_step(s):
        gy_came(0, s).wait_recv()
        if s < HALF_Y - 1:
            gy_came(1, s).wait_recv()
        along_y(s + 1)
        along_z(came_at[s + 1])
        along_x(came_at[s])

    def to_sibling(rows):
        for r in rows:
            for j in range(NX - 1):
                gx_came(r, j).wait_recv()
            gs_copy(r).start()

    wc_copy.wait()
    ws_copy.wait()
    row = lax.broadcasted_iota(jnp.int32, (ROWS, HB), 0)
    col = lax.broadcasted_iota(jnp.int32, (ROWS, HB), 1)
    spread = jnp.broadcast_to(ws[...].astype(jnp.float32), (ROWS, HB))
    w_scale = jnp.sum(jnp.where(row // 2 == col, spread, 0.0), axis=1, keepdims=True)
    wc[...] = (wc[...].astype(jnp.float32) * w_scale).astype(jnp.bfloat16)
    quarter = ROWS // NX
    w_buf[y, z, core, x] = wc[pl.ds(pl.multiple_of(x * quarter, quarter), quarter)]

    def enter():
        pl.semaphore_wait(barrier, len(near) + zh)
        sib_copy(0).start()
        for zh_ in range(NZH - 1):
            @pl.when(zh_ < zh)
            def _():
                signal(later_h, h_peer(zh_))
        along_y(0)
        along_z((0,))

    cot_copy.wait()
    compute(0)
    compute(1, enter)
    sib_copy(0).wait_recv()
    pass_on(0, 0, 0)
    pass_on(1, 0, 1)
    compute(2)
    sib_copy(1).wait_recv()
    pass_on(0, 1, 1)
    compute(3)
    sib_copy(2).wait_recv()
    pass_on(1, 1, 0)
    g_step(0)
    compute(4)
    sib_copy(3).wait_recv()
    pass_on(0, 1, 0)
    pass_on(1, 1, 1)
    compute(5)
    sib_copy(4).wait_recv()
    pass_on(0, 2, 1)
    pass_on(1, 2, 0)
    compute(6)
    sib_copy(5).wait_recv()
    pass_on(0, 2, 0)
    pass_on(1, 2, 1)
    g_step(1)
    compute(7)
    sib_copy(6).wait_recv()
    pass_on(0, 3, 1)
    pass_on(1, 3, 0)
    pass_on(0, 3, 0)
    pass_on(1, 3, 1)
    sib_copy(7).wait_recv()

    g_step(2)

    last = HALF_Y - 1

    def z_copy(z_):
        return remote(z_out.at[z_], z_in.at[z], z_ss.at[z_], z_rs.at[z], at(y, z_, core))

    def z_came(z_):
        return remote(z_out.at[z_], z_in.at[z_], z_ss.at[z_], z_rs.at[z_], sibling)

    for q in range(NZ):
        ring_copy(0, last, q).wait_recv()
        ring_copy(1, last, q).wait_recv()
        total = own[NY - 1, q] + sib_in[NY - 1, q].astype(jnp.float32)
        total += r_in[last, q].astype(jnp.float32) + l_in[last, q].astype(jnp.float32)
        own[NY - 1, q] = total
        z_out[q] = total.astype(jnp.bfloat16)

        @pl.when(q != z)
        def _():
            z_copy(q).start()

    g_step(3)

    node_total = own[NY - 1, z]
    for j in range(1, NZ):
        z_ = (z + j) % NZ
        z_came(z_).wait_recv()
        node_total += z_in[z_].astype(jnp.float32)
    even, odd = node_total[:HB], node_total[HB:]
    scale = block_scale(even, odd, NODE_TOP)
    inverse = 1.0 / scale
    for at_row, value in ((0, even), (HB, odd)):
        codes = (value * inverse).astype(jnp.bfloat16)
        h_buf[zh, at_row:at_row + HB] = (codes.astype(jnp.float32) * scale).astype(jnp.bfloat16)

    def h_copy(j):
        return remote(
            h_buf.at[zh], h_buf.at[zh], h_ss.at[j], h_rs.at[j], h_peer((zh + j + 1) % NZH)
        )

    def h_came(j):
        dst = h_buf.at[(zh + NZH - 1 - j) % NZH]
        return remote(dst, dst, h_ss.at[j], h_rs.at[j], sibling)

    @pl.when(zh < NZH - 1)
    def _():
        pl.semaphore_wait(later_h, NZH - 1 - zh)

    for j in range(NZH - 1):
        h_copy(j).start()

    along_x(came_at[HALF_Y])
    to_sibling(near_rows)

    def term(r):
        gs_came(r).wait_recv()
        b = (y + r) % NY
        dense = w_buf[b].reshape(CHUNK, HD)
        cols = pl.ds(pl.multiple_of(b * CHUNK, CHUNK), CHUNK)
        return jnp.dot(tok[:, cols], dense, preferred_element_type=jnp.float32)

    for k in range(NY):
        sib_copy(k).wait_send()
        for j in range(NZ - 1):
            gz_copy(k, j).wait_send()
    for s in range(HALF_Y):
        for q in range(NZ):
            for way in range(2):
                if s > 0 or q in ways[way]:
                    ring_copy(way, s, q).wait_send()
    for s in range(HALF_Y):
        gy_copy(0, s).wait_send()
    for s in range(HALF_Y - 1):
        gy_copy(1, s).wait_send()
    for j in range(NZ - 1):
        z_copy((z + j + 1) % NZ).wait_send()

    for j in range(NZH - 1):
        h_came(j).wait_recv()
    summed = h_buf[0].astype(jnp.float32)
    for i in range(1, NZH):
        summed += h_buf[i].astype(jnp.float32)
    x_buf[x] = summed.astype(jnp.bfloat16)

    def x_copy(j):
        return remote(x_buf.at[x], x_buf.at[x], x_ss.at[j], x_rs.at[j], x_peers[j])

    def x_came(j):
        dst = x_buf.at[(x + NX - 1 - j) % NX]
        return remote(dst, dst, x_ss.at[j], x_rs.at[j], sibling)

    for j in range(NX - 1):
        x_copy(j).start()

    to_sibling(far_rows)
    projected = term(0)
    for r in near_rows[1:]:
        projected += term(r)
    for k in range(NY):
        for j in range(NX - 1):
            gx_copy(k, j).wait_send()
    for r in far_rows:
        projected += term(r)
    proj_ref[...] = projected.astype(jnp.bfloat16)
    for k in range(NY):
        gs_copy(k).wait_send()
    for j in range(NZH - 1):
        h_copy(j).wait_send()

    for j in range(NX - 1):
        x_came(j).wait_recv()
    summed = x_buf[0].astype(jnp.float32)
    for i in range(1, NX):
        summed += x_buf[i].astype(jnp.float32)
    grad_ref[pl.ds(0, HB, stride=2), :] = summed[:HB]
    grad_ref[pl.ds(1, HB, stride=2), :] = summed[HB:]
    for j in range(NX - 1):
        x_copy(j).wait_send()


def settle(p_ref, g_ref, proj_ref, grad_ref):
    proj_ref[...] = p_ref[...]
    grad_ref[...] = g_ref[...]


def on_device(tokens, cotangent, weight_codes, weight_scales, rounding_table, stream_offsets):
    dma = pltpu.SemaphoreType.DMA
    bf16, f32 = jnp.bfloat16, jnp.float32
    column = (NZ, ROWS, HD)
    scratch = [
        pltpu.VMEM((TOK, NY * CHUNK), bf16),
        pltpu.VMEM((TOK, HD), bf16),
        pltpu.VMEM((ROWS, HD), bf16),
        pltpu.VMEM((1, HB), bf16),
        pltpu.VMEM((NY * CHUNK, HD), jnp.int32),
        pltpu.VMEM((CHUNK, HD), f32),
        pltpu.VMEM((NY,) + column, f32),
        pltpu.VMEM((NY,) + column, bf16),
        pltpu.VMEM((NY,) + column, bf16),
        pltpu.VMEM((HALF_Y,) + column, bf16),
        pltpu.VMEM((HALF_Y,) + column, bf16),
        pltpu.VMEM((HALF_Y,) + column, bf16),
        pltpu.VMEM((HALF_Y,) + column, bf16),
        pltpu.VMEM(column, bf16),
        pltpu.VMEM(column, bf16),
        pltpu.VMEM((NZH, ROWS, HD), bf16),
        pltpu.VMEM((NX, ROWS, HD), bf16),
        pltpu.VMEM((NY, NZ, 2, NX, ROWS // NX, HD), bf16),
        dma((NY,)), dma((NY,)), dma((3,)), dma((NY,)), dma((NY,)),
        dma((HALF_Y, NZ)), dma((HALF_Y, NZ)), dma((HALF_Y, NZ)), dma((HALF_Y, NZ)),
        dma((NZ,)), dma((NZ,)), dma((NZH - 1,)), dma((NZH - 1,)), dma((NX - 1,)), dma((NX - 1,)),
        dma((NY, NZ - 1)), dma((NY, NZ - 1)),
        dma((HALF_Y,)), dma((HALF_Y,)), dma((HALF_Y,)), dma((HALF_Y,)),
        dma((NY, NX - 1)), dma((NY, NX - 1)),
        dma((NY,)), dma((NY,)),
        pltpu.SemaphoreType.REGULAR,
    ]
    hbm = pl.BlockSpec(memory_space=pltpu.MemorySpace.HBM)
    vmem = pl.BlockSpec(memory_space=pltpu.VMEM)
    out_shape = (
        jax.ShapeDtypeStruct((TOK, HD), bf16),
        jax.ShapeDtypeStruct((ROWS, HD), f32),
    )
    results = pl.pallas_call(
        kernel,
        out_shape=out_shape,
        in_specs=[hbm, hbm, hbm, hbm, hbm, pl.BlockSpec(memory_space=pltpu.SMEM)],
        out_specs=(vmem, vmem),
        scratch_shapes=scratch,
        compiler_params=pltpu.CompilerParams(
            collective_id=0, has_side_effects=True, vmem_limit_bytes=VMEM_LIMIT
        ),
        cost_estimate=pl.CostEstimate(
            flops=4 * TOK * NY * CHUNK * HD, bytes_accessed=9 * 2**20, transcendentals=0
        ),
    )(tokens, cotangent, weight_codes, weight_scales.reshape(1, HB), rounding_table, stream_offsets)
    return pl.pallas_call(
        settle,
        out_shape=out_shape,
        in_specs=[vmem, vmem],
        out_specs=(vmem, vmem),
        compiler_params=pltpu.CompilerParams(vmem_limit_bytes=VMEM_LIMIT),
    )(*results)


def solution(mesh):
    assert dict(mesh.shape) == {"node": NX * NZH, "local": NY * NZ * 2}
    in_specs = (
        P(("node", "local"), None),
        P(("node", "local"), None),
        P("local", None),
        P("local"),
        P(),
        P(("node", "local")),
    )
    out_specs = (P(("node", "local"), None), P("local", None))
    return jax.shard_map(
        on_device, mesh=mesh, in_specs=in_specs, out_specs=out_specs, check_vma=False
    )
```

```python
import jax
import jax.numpy as jnp
from jax import lax
from jax.experimental import pallas as pl
from jax.experimental.pallas import tpu as pltpu
from jax.sharding import PartitionSpec as P

MESH = pl.DeviceIdType.MESH
EPS = 1e-06
HEADROOM = 1.0078125
GRAD_TOP = 7.0
NODE_TOP = 127.0

NX, NZH, NY, NZ = 4, 3, 8, 4
HALF_Y = NY // 2
ROWS = 128
HD = 128
HB = ROWS // 2
CHUNK = NZ * 2 * ROWS
TOK = 256
HALF_Z = NZ // 2
VMEM_LIMIT = 60 * 2**20
AHEAD = 3


def block_scale(even, odd, top):
    largest = jnp.max(jnp.maximum(jnp.abs(even), jnp.abs(odd)), axis=1, keepdims=True)
    return ((largest + EPS) * HEADROOM / top).astype(jnp.bfloat16).astype(jnp.float32)


def kernel(
    tok_hbm, cot_hbm, wc_hbm, ws_hbm, table_hbm, off_ref,
    proj_ref, grad_ref,
    tok, cot, wc, ws, table, part, own, sib_out, sib_in, r_out, r_in, l_out, l_in,
    z_out, z_in, h_buf, x_buf, w_buf,
    tok_sem, table_sem, small_sem, sib_ss, sib_rs, r_ss, r_rs, l_ss, l_rs,
    z_ss, z_rs, h_ss, h_rs, x_ss, x_rs, gz_ss, gz_rs, gr_ss, gr_rs, gl_ss, gl_rs,
    gx_ss, gx_rs, gs_ss, gs_rs, later_h,
):
    node = lax.axis_index("node")
    local = lax.axis_index("local")
    x, zh = node // NZH, node % NZH
    y, z, core = local // (NZ * 2), (local // 2) % NZ, local % 2
    other = 1 - core

    def at(y_, z_, c_):
        return (node, (y_ * NZ + z_) * 2 + c_)

    def up(step):
        return at((y + step) % NY, z, core)

    def down(step):
        return at((y + NY - step) % NY, z, core)

    sibling = at(y, z, other)
    x_peers = [(((x + j) % NX) * NZH + zh, local) for j in range(1, NX)]
    z_peers = [at(y, (z + j) % NZ, core) for j in range(1, NZ)]
    near = [sibling, up(1), down(1)] + z_peers + x_peers

    def h_peer(zh_):
        return (x * NZH + zh_, local)

    def signal(sem, peer):
        pl.semaphore_signal(sem, inc=1, device_id=peer, device_id_type=MESH)

    barrier = pltpu.get_barrier_semaphore()
    for peer in near:
        signal(barrier, peer)
    for zh_ in range(1, NZH):
        @pl.when(zh < zh_)
        def _():
            signal(barrier, h_peer(zh_))

    order = [(y + HALF_Y) % NY]
    for far in range(HALF_Y - 1, 0, -1):
        order += [(y + far) % NY, (y + NY - far) % NY]
    order += [y]

    def tok_copy(k):
        cols = pl.ds(pl.multiple_of(order[k] * CHUNK, CHUNK), CHUNK)
        return pltpu.make_async_copy(tok_hbm.at[:, cols], tok.at[:, cols], tok_sem.at[k])

    def table_copy(k):
        rows = pl.ds(pl.multiple_of(order[k] * CHUNK, CHUNK), CHUNK)
        return pltpu.make_async_copy(table_hbm.at[rows], table.at[rows], table_sem.at[k])

    def fetch(k):
        tok_copy(k).start()
        table_copy(k).start()

    cot_copy = pltpu.make_async_copy(cot_hbm, cot, small_sem.at[0])
    wc_copy = pltpu.make_async_copy(wc_hbm, wc, small_sem.at[1])
    ws_copy = pltpu.make_async_copy(ws_hbm, ws, small_sem.at[2])
    cot_copy.start()
    fetch(0)
    wc_copy.start()
    ws_copy.start()
    for k in range(1, AHEAD):
        fetch(k)

    def remote(src, dst, ss, rs, dev):
        return pltpu.make_async_remote_copy(
            src_ref=src, dst_ref=dst, send_sem=ss, recv_sem=rs, device_id=dev, device_id_type=MESH
        )

    offset = off_ref[0]

    def quantized(block, core_of, base):
        start = pl.multiple_of((block * 2 + core_of) * ROWS, ROWS)
        even = part[pl.ds(start, HB, stride=2), :]
        odd = part[pl.ds(start + 1, HB, stride=2), :]
        scale = block_scale(even, odd, GRAD_TOP)
        inverse = 1.0 / scale
        out = []
        for parity, value in ((0, even), (1, odd)):
            draws = table[pl.ds(base + start + parity, HB, stride=2), :]
            draws = ((draws + offset) & 1023).astype(jnp.float32)
            shift = draws * (1.0 / 1024.0) + (0.5 / 1024.0 - 0.5)
            codes = (value * inverse + shift).astype(jnp.bfloat16)
            out.append(codes.astype(jnp.float32) * scale)
        return out

    def sib_copy(k):
        return remote(sib_out.at[k], sib_in.at[k], sib_ss.at[k], sib_rs.at[k], sibling)

    def compute(k, ready=None):
        tok_copy(k).wait()
        table_copy(k).wait()
        if k + AHEAD < NY:
            fetch(k + AHEAD)
        base = pl.multiple_of(order[k] * CHUNK, CHUNK)
        part[...] = lax.dot_general(
            tok[:, pl.ds(base, CHUNK)], cot[...], (((0,), (0,)), ((), ())),
            preferred_element_type=jnp.float32,
        )
        for block in range(NZ):
            even, odd = quantized(block, other, base)
            sib_out[k, block, :HB] = even.astype(jnp.bfloat16)
            sib_out[k, block, HB:] = odd.astype(jnp.bfloat16)
        if ready is not None:
            ready()
        if k > 0:
            sib_copy(k).start()
        for block in range(NZ):
            even, odd = quantized(block, core, base)
            own[k, block, :HB] = even
            own[k, block, HB:] = odd

    def ring_copy(way, s, q):
        out, came, ss, rs, dev = (
            (r_out, r_in, r_ss, r_rs, up(1)) if way == 0 else (l_out, l_in, l_ss, l_rs, down(1))
        )
        return remote(out.at[s, q], came.at[s, q], ss.at[s, q], rs.at[s, q], dev)

    ways = (range(HALF_Z), range(HALF_Z, NZ))

    def pass_on(way, s, part_of):
        k = 0 if s == 0 else 2 * s - 1 + way
        out, came = (r_out, r_in) if way == 0 else (l_out, l_in)
        for q in ways[part_of]:
            total = own[k, q] + sib_in[k, q].astype(jnp.float32)
            if s > 1 or (s == 1 and part_of == way):
                ring_copy(way, s - 1, q).wait_recv()
                total += came[s - 1, q].astype(jnp.float32)
            out[s, q] = total.astype(jnp.bfloat16)
            ring_copy(way, s, q).start()

    def gy_copy(way, s):
        if way == 0:
            piece = w_buf.at[(y + NY - s) % NY, z, core, x]
            return remote(piece, piece, gr_ss.at[s], gr_rs.at[s], up(1))
        piece = w_buf.at[(y + s) % NY, z, core, x]
        return remote(piece, piece, gl_ss.at[s], gl_rs.at[s], down(1))

    def gy_came(way, s):
        if way == 0:
            piece = w_buf.at[(y + NY - s - 1) % NY, z, core, x]
            return remote(piece, piece, gr_ss.at[s], gr_rs.at[s], sibling)
        piece = w_buf.at[(y + s + 1) % NY, z, core, x]
        return remote(piece, piece, gl_ss.at[s], gl_rs.at[s], sibling)

    def gz_copy(r, j):
        piece = w_buf.at[(y + r) % NY, z, core, x]
        return remote(piece, piece, gz_ss.at[r, j], gz_rs.at[r, j], z_peers[j])

    def gz_came(r, j):
        piece = w_buf.at[(y + r) % NY, (z + NZ - 1 - j) % NZ, core, x]
        return remote(piece, piece, gz_ss.at[r, j], gz_rs.at[r, j], sibling)

    def gx_copy(r, j):
        piece = w_buf.at[(y + r) % NY, :, core, x]
        return remote(piece, piece, gx_ss.at[r, j], gx_rs.at[r, j], x_peers[j])

    def gx_came(r, j):
        piece = w_buf.at[(y + r) % NY, :, core, (x + NX - 1 - j) % NX]
        return remote(piece, piece, gx_ss.at[r, j], gx_rs.at[r, j], sibling)

    def gs_copy(r):
        piece = w_buf.at[(y + r) % NY, :, core]
        return remote(piece, piece, gs_ss.at[r], gs_rs.at[r], sibling)

    def gs_came(r):
        piece = w_buf.at[(y + r) % NY, :, other]
        return remote(piece, piece, gs_ss.at[r], gs_rs.at[r], sibling)

    def along_y(s):
        if s < HALF_Y:
            gy_copy(0, s).start()
        if s < HALF_Y - 1:
            gy_copy(1, s).start()

    def along_z(rows):
        for r in rows:
            for j in range(NZ - 1):
                gz_copy(r, j).start()

    def along_x(rows):
        for r in rows:
            for j in range(NZ - 1):
                gz_came(r, j).wait_recv()
            for j in range(NX - 1):
                gx_copy(r, j).start()

    near_rows, far_rows = (0, NY - 1, 1, NY - 2, 2), (NY - 3, 3, HALF_Y)

    came_at = ((0,), (NY - 1, 1), (NY - 2, 2), (NY - 3, 3), (HALF_Y,))

    def g_step(s):
        gy_came(0, s).wait_recv()
        if s < HALF_Y - 1:
            gy_came(1, s).wait_recv()
        along_y(s + 1)
        along_z(came_at[s + 1])
        along_x(came_at[s])

    def to_sibling(rows):
        for r in rows:
            for j in range(NX - 1):
                gx_came(r, j).wait_recv()
            gs_copy(r).start()

    wc_copy.wait()
    ws_copy.wait()
    row = lax.broadcasted_iota(jnp.int32, (ROWS, HB), 0)
    col = lax.broadcasted_iota(jnp.int32, (ROWS, HB), 1)
    spread = jnp.broadcast_to(ws[...].astype(jnp.float32), (ROWS, HB))
    w_scale = jnp.sum(jnp.where(row // 2 == col, spread, 0.0), axis=1, keepdims=True)
    wc[...] = (wc[...].astype(jnp.float32) * w_scale).astype(jnp.bfloat16)
    quarter = ROWS // NX
    w_buf[y, z, core, x] = wc[pl.ds(pl.multiple_of(x * quarter, quarter), quarter)]

    def enter():
        pl.semaphore_wait(barrier, len(near) + zh)
        sib_copy(0).start()
        for zh_ in range(NZH - 1):
            @pl.when(zh_ < zh)
            def _():
                signal(later_h, h_peer(zh_))
        along_y(0)
        along_z((0,))

    cot_copy.wait()
    compute(0)
    compute(1, enter)
    sib_copy(0).wait_recv()
    pass_on(0, 0, 0)
    pass_on(1, 0, 1)
    compute(2)
    sib_copy(1).wait_recv()
    pass_on(0, 1, 1)
    compute(3)
    sib_copy(2).wait_recv()
    pass_on(1, 1, 0)
    g_step(0)
    compute(4)
    sib_copy(3).wait_recv()
    pass_on(0, 1, 0)
    pass_on(1, 1, 1)
    compute(5)
    sib_copy(4).wait_recv()
    pass_on(0, 2, 1)
    pass_on(1, 2, 0)
    compute(6)
    sib_copy(5).wait_recv()
    pass_on(0, 2, 0)
    pass_on(1, 2, 1)
    g_step(1)
    compute(7)
    sib_copy(6).wait_recv()
    pass_on(0, 3, 1)
    pass_on(1, 3, 0)
    pass_on(0, 3, 0)
    pass_on(1, 3, 1)
    sib_copy(7).wait_recv()

    g_step(2)

    last = HALF_Y - 1

    def z_copy(z_):
        return remote(z_out.at[z_], z_in.at[z], z_ss.at[z_], z_rs.at[z], at(y, z_, core))

    def z_came(z_):
        return remote(z_out.at[z_], z_in.at[z_], z_ss.at[z_], z_rs.at[z_], sibling)

    for q in range(NZ):
        ring_copy(0, last, q).wait_recv()
        ring_copy(1, last, q).wait_recv()
        total = own[NY - 1, q] + sib_in[NY - 1, q].astype(jnp.float32)
        total += r_in[last, q].astype(jnp.float32) + l_in[last, q].astype(jnp.float32)
        own[NY - 1, q] = total
        z_out[q] = total.astype(jnp.bfloat16)

        @pl.when(q != z)
        def _():
            z_copy(q).start()

    g_step(3)

    node_total = own[NY - 1, z]
    for j in range(1, NZ):
        z_ = (z + j) % NZ
        z_came(z_).wait_recv()
        node_total += z_in[z_].astype(jnp.float32)
    even, odd = node_total[:HB], node_total[HB:]
    scale = block_scale(even, odd, NODE_TOP)
    inverse = 1.0 / scale
    parities = range(2)
    for p, value in zip(parities, (even, odd)):
        codes = (value * inverse).astype(jnp.bfloat16)
        h_buf[zh, p] = (codes.astype(jnp.float32) * scale).astype(jnp.bfloat16)

    def h_copy(j, p):
        mine = h_buf.at[zh, p]
        return remote(mine, mine, h_ss.at[j, p], h_rs.at[j, p], h_peer((zh + j + 1) % NZH))

    def h_came(j, p):
        dst = h_buf.at[(zh + NZH - 1 - j) % NZH, p]
        return remote(dst, dst, h_ss.at[j, p], h_rs.at[j, p], sibling)

    @pl.when(zh < NZH - 1)
    def _():
        pl.semaphore_wait(later_h, NZH - 1 - zh)

    for p in parities:
        for j in range(NZH - 1):
            h_copy(j, p).start()

    along_x(came_at[HALF_Y])
    to_sibling(near_rows)

    def term(r):
        gs_came(r).wait_recv()
        b = (y + r) % NY
        dense = w_buf[b].reshape(CHUNK, HD)
        cols = pl.ds(pl.multiple_of(b * CHUNK, CHUNK), CHUNK)
        return jnp.dot(tok[:, cols], dense, preferred_element_type=jnp.float32)

    for k in range(NY):
        sib_copy(k).wait_send()
        for j in range(NZ - 1):
            gz_copy(k, j).wait_send()
    for s in range(HALF_Y):
        for q in range(NZ):
            for way in range(2):
                if s > 0 or q in ways[way]:
                    ring_copy(way, s, q).wait_send()
    for s in range(HALF_Y):
        gy_copy(0, s).wait_send()
    for s in range(HALF_Y - 1):
        gy_copy(1, s).wait_send()
    for j in range(NZ - 1):
        z_copy((z + j + 1) % NZ).wait_send()

    def x_copy(j, p):
        mine = x_buf.at[x, p]
        return remote(mine, mine, x_ss.at[j, p], x_rs.at[j, p], x_peers[j])

    def x_came(j, p):
        dst = x_buf.at[(x + NX - 1 - j) % NX, p]
        return remote(dst, dst, x_ss.at[j, p], x_rs.at[j, p], sibling)

    for p in parities:
        for j in range(NZH - 1):
            h_came(j, p).wait_recv()
        summed = h_buf[0, p].astype(jnp.float32)
        for i in range(1, NZH):
            summed += h_buf[i, p].astype(jnp.float32)
        x_buf[x, p] = summed.astype(jnp.bfloat16)
        for j in range(NX - 1):
            x_copy(j, p).start()

    to_sibling(far_rows)
    projected = term(0)
    for r in near_rows[1:]:
        projected += term(r)
    for k in range(NY):
        for j in range(NX - 1):
            gx_copy(k, j).wait_send()
    for r in far_rows:
        projected += term(r)
    proj_ref[...] = projected.astype(jnp.bfloat16)
    for k in range(NY):
        gs_copy(k).wait_send()
    for p in parities:
        for j in range(NZH - 1):
            h_copy(j, p).wait_send()

    for p in parities:
        for j in range(NX - 1):
            x_came(j, p).wait_recv()
        summed = x_buf[0, p].astype(jnp.float32)
        for i in range(1, NX):
            summed += x_buf[i, p].astype(jnp.float32)
        grad_ref[pl.ds(p, HB, stride=2), :] = summed
    for p in parities:
        for j in range(NX - 1):
            x_copy(j, p).wait_send()


def settle(p_ref, g_ref, proj_ref, grad_ref):
    proj_ref[...] = p_ref[...]
    grad_ref[...] = g_ref[...]


def on_device(tokens, cotangent, weight_codes, weight_scales, rounding_table, stream_offsets):
    dma = pltpu.SemaphoreType.DMA
    bf16, f32 = jnp.bfloat16, jnp.float32
    column = (NZ, ROWS, HD)
    scratch = [
        pltpu.VMEM((TOK, NY * CHUNK), bf16),
        pltpu.VMEM((TOK, HD), bf16),
        pltpu.VMEM((ROWS, HD), bf16),
        pltpu.VMEM((1, HB), bf16),
        pltpu.VMEM((NY * CHUNK, HD), jnp.int32),
        pltpu.VMEM((CHUNK, HD), f32),
        pltpu.VMEM((NY,) + column, f32),
        pltpu.VMEM((NY,) + column, bf16),
        pltpu.VMEM((NY,) + column, bf16),
        pltpu.VMEM((HALF_Y,) + column, bf16),
        pltpu.VMEM((HALF_Y,) + column, bf16),
        pltpu.VMEM((HALF_Y,) + column, bf16),
        pltpu.VMEM((HALF_Y,) + column, bf16),
        pltpu.VMEM(column, bf16),
        pltpu.VMEM(column, bf16),
        pltpu.VMEM((NZH, 2, HB, HD), bf16),
        pltpu.VMEM((NX, 2, HB, HD), bf16),
        pltpu.VMEM((NY, NZ, 2, NX, ROWS // NX, HD), bf16),
        dma((NY,)), dma((NY,)), dma((3,)), dma((NY,)), dma((NY,)),
        dma((HALF_Y, NZ)), dma((HALF_Y, NZ)), dma((HALF_Y, NZ)), dma((HALF_Y, NZ)),
        dma((NZ,)), dma((NZ,)), dma((NZH - 1, 2)), dma((NZH - 1, 2)), dma((NX - 1, 2)), dma((NX - 1, 2)),
        dma((NY, NZ - 1)), dma((NY, NZ - 1)),
        dma((HALF_Y,)), dma((HALF_Y,)), dma((HALF_Y,)), dma((HALF_Y,)),
        dma((NY, NX - 1)), dma((NY, NX - 1)),
        dma((NY,)), dma((NY,)),
        pltpu.SemaphoreType.REGULAR,
    ]
    hbm = pl.BlockSpec(memory_space=pltpu.MemorySpace.HBM)
    vmem = pl.BlockSpec(memory_space=pltpu.VMEM)
    out_shape = (
        jax.ShapeDtypeStruct((TOK, HD), bf16),
        jax.ShapeDtypeStruct((ROWS, HD), f32),
    )
    results = pl.pallas_call(
        kernel,
        out_shape=out_shape,
        in_specs=[hbm, hbm, hbm, hbm, hbm, pl.BlockSpec(memory_space=pltpu.SMEM)],
        out_specs=(vmem, vmem),
        scratch_shapes=scratch,
        compiler_params=pltpu.CompilerParams(
            collective_id=0, has_side_effects=True, vmem_limit_bytes=VMEM_LIMIT
        ),
        cost_estimate=pl.CostEstimate(
            flops=4 * TOK * NY * CHUNK * HD, bytes_accessed=9 * 2**20, transcendentals=0
        ),
    )(tokens, cotangent, weight_codes, weight_scales.reshape(1, HB), rounding_table, stream_offsets)
    return pl.pallas_call(
        settle,
        out_shape=out_shape,
        in_specs=[vmem, vmem],
        out_specs=(vmem, vmem),
        compiler_params=pltpu.CompilerParams(vmem_limit_bytes=VMEM_LIMIT),
    )(*results)


def solution(mesh):
    assert dict(mesh.shape) == {"node": NX * NZH, "local": NY * NZ * 2}
    in_specs = (
        P(("node", "local"), None),
        P(("node", "local"), None),
        P("local", None),
        P("local"),
        P(),
        P(("node", "local")),
    )
    out_specs = (P(("node", "local"), None), P("local", None))
    return jax.shard_map(
        on_device, mesh=mesh, in_specs=in_specs, out_specs=out_specs, check_vma=False
    )
```
